128 devices in a mesh: row: 16 (over y, x), col: 8 (over z, core).
Axes of the slice: x: 4, y: 4, z: 4, core: 2. Of those that a mesh axis runs over, the one named last changes fastest.
Arguments:
- statistic: float32 [16384, 16384], P('row', 'col'), may hold values from -6 to 6
- noise: bfloat16 [16384, 16384], P('row', 'col'), may hold values from -12 to 12
- grads: bfloat16 [16384, 4096], P('row', 'col'), may hold values from -1.5 to 1.5
Outputs:
- updated: float32 [16384, 16384], P('row', 'col')
The draws below stay inside these ranges and needn't reach their ends.
All inputs are finite; a program needn't handle non-finite values.
Results may differ from the reference program's by a relative error of at most 0.0003.
Values may be sent and summed in bfloat16 or wider, within the bound.
No kernel may reach another device: no remote copies, remote signals or barrier semaphores. Data moves between devices by JAX's collectives and lax.ppermute only.
A program may use at most 640 MiB of HBM per device.

```python
import jax
import jax.numpy as jnp
from jax import lax

M = 16384
K = 4096
N_ROW = 16


def block_scale(stream_key, shape, cuts, low, high):
    def one(dim, parts):
        steps = jax.random.uniform(jax.random.fold_in(jax.random.fold_in(stream_key, 6), dim), (parts,), jnp.float32, low / len(cuts), high / len(cuts))
        return jnp.repeat(jnp.exp(steps), shape[dim] // parts).reshape((-1,) + (1,) * (len(shape) - dim - 1))

    factor_of = one(*cuts[0])
    for cut in cuts[1:]:
        factor_of = factor_of * one(*cut)
    return factor_of


def gaussian(key, dims, width, most, shards=(), kind=jnp.bfloat16):
    array = jax.random.normal(key, dims, jnp.float32) * width
    if len(shards) > 0:
        array = block_scale(key, dims, shards, -0.22, 0.18) * array
    return jnp.clip(array, min=-most, max=most).astype(kind)


def setup_inputs(seed: int = 0) -> dict:
    key_of = jax.random.split(jax.random.key(seed), 4)
    return {
        "statistic": gaussian(key_of[0], (M, M), 1.0, 6.0, ((0, 16), (1, 8)), jnp.float32),
        "noise": gaussian(key_of[1], (M, M), 2.0, 12.0, ((0, 16), (1, 8))),
        "grads": gaussian(key_of[2], (M, K), 0.25, 1.5, ((0, 16), (1, 8))),
    }


def reference(statistic, noise, grads):
    block = M // N_ROW
    pieces = grads.reshape(N_ROW, block, K)

    def one_block(piece):
        return jnp.dot(piece, grads.T, preferred_element_type=jnp.float32)

    product = lax.map(one_block, pieces).reshape(M, M)
    rows = jnp.arange(M, dtype=jnp.int32)[:, None]
    cols = jnp.arange(M, dtype=jnp.int32)[None, :]
    blended = 0.9 * statistic + 0.1 * (product + noise.astype(jnp.float32))
    return jnp.where(rows >= cols, blended, jnp.zeros_like(blended))
```

```python
import functools

import jax
import jax.numpy as jnp
from jax import lax
from jax.experimental import pallas as pl
from jax.experimental.pallas import tpu as pltpu
from jax.sharding import PartitionSpec as P

AXES = ("row", "col")
SIDE = 4
ORDER = (0, 1, 3, 2)
ROWS_TILE = 256
STREAMS = 2


def place(y, x, z, core):
    return (y % SIDE * SIDE + x % SIDE) * 2 * SIDE + z % SIDE * 2 + core


def coords():
    for y in range(SIDE):
        for x in range(SIDE):
            for z in range(SIDE):
                for core in range(2):
                    yield y, x, z, core


def turn(t):
    return t if t % 2 else (t + 2) % SIDE


def spread_pairs():
    pairs = []
    for y, x, z, core in coords():
        half = x // 2
        to_x = x if core == half else SIDE - 1 - x
        pairs.append((place(y, x, z, core), place(y + turn((z - y) % SIDE), to_x, y, half)))
    return pairs


def shift_pairs(step, first):
    pairs = []
    for y, x, z, core in coords():
        along_x = (core == 0) == first
        to = place(y, x - step, z, core) if along_x else place(y - step, x, z, core)
        pairs.append((place(y, x, z, core), to))
    return pairs


def unit_table():
    row, col = lax.axis_index("row"), lax.axis_index("col")
    y, x, z, core = row // SIDE, row % SIDE, col // 2, col % 2
    blocks, eighths = [], []
    for j in range(SIDE):
        for i in range(SIDE):
            uy = (y + jnp.where(core == 0, j, i)) % SIDE
            ux = (x + jnp.where(core == 0, i, j)) % SIDE
            t = (uy - z) % SIDE
            k = (z + jnp.where(t % 2 == 1, t, (t + 2) % SIDE)) % SIDE
            home = ux // 2 == core
            source_x = jnp.where(home, ux, SIDE - 1 - ux)
            blocks.append(source_x % 2)
            eighths.append(2 * k + jnp.where(home, core, 1 - core))
    return jnp.stack(blocks + eighths + [row, col]).astype(jnp.int32)


def product_kernel(stream, table, panel, statistic, noise, own, ahead, behind, low, high, *refs):
    out, weights, sems = refs[-3:]
    tile, width = out.shape
    depth = own.shape[-1]
    m, b = pl.program_id(0), pl.program_id(1)
    sources = [(0, i, own.at[s]) for s, i in enumerate(ORDER)]
    sources += [(1, i, ahead.at[s]) for s, i in enumerate(ORDER)]
    sources += [(3, i, behind.at[s]) for s, i in enumerate(ORDER)]
    sources += [(2, i, low.at[s]) for s, i in enumerate(ORDER[:2])]
    sources += [(2, i, high.at[s]) for s, i in enumerate(ORDER[2:])]

    @pl.when((m == 0) & (b == 0))
    def _():
        for j, i, source in sources:
            block, eighth = table[j * SIDE + i], table[16 + j * SIDE + i]
            at = pl.ds(pl.multiple_of(eighth * depth, depth), depth)
            pltpu.make_async_copy(source, weights.at[block, :, at], sems.at[block, eighth]).start()

    @pl.when(m == 0)
    def _():
        for eighth in range(8):
            at = pl.ds(eighth * depth, depth)
            pltpu.make_async_copy(own.at[0], weights.at[b, :, at], sems.at[b, eighth]).wait()

    product = lax.dot_general(
        panel[...], weights[b], (((1,), (1,)), ((), ())), preferred_element_type=jnp.float32
    )
    blended = 0.9 * statistic[...] + 0.1 * (product + noise[...].astype(jnp.float32))
    rows = table[32] * (tile * pl.num_programs(0)) + m * tile
    rows = rows + lax.broadcasted_iota(jnp.int32, (tile, width), 0)
    cols = (table[33] * 2 + b) * (width * STREAMS) + stream * width
    cols = cols + lax.broadcasted_iota(jnp.int32, (tile, width), 1)
    out[...] = jnp.where(rows >= cols, blended, 0.0)


def blend(stream, table, panel, statistic, noise, pieces, before):
    rows, depth = panel.shape
    width = pieces[0].shape[1]
    spec = pl.BlockSpec((ROWS_TILE, width), lambda m, b, t: (m, STREAMS * b + stream))
    anywhere = pl.BlockSpec(memory_space=pl.ANY)
    earlier = [] if before is None else [before]
    return pl.pallas_call(
        functools.partial(product_kernel, stream),
        grid_spec=pltpu.PrefetchScalarGridSpec(
            num_scalar_prefetch=1,
            grid=(rows // ROWS_TILE, 2),
            in_specs=[pl.BlockSpec((ROWS_TILE, depth), lambda m, b, t: (m, 0)), spec, spec]
            + [anywhere] * (len(pieces) + len(earlier)),
            out_specs=spec,
            scratch_shapes=[
                pltpu.VMEM((2, width, depth), jnp.bfloat16),
                pltpu.SemaphoreType.DMA((2, 8)),
            ],
        ),
        out_shape=jax.ShapeDtypeStruct(statistic.shape, jnp.float32),
        input_output_aliases={} if before is None else {4 + len(pieces): 0},
        compiler_params=pltpu.CompilerParams(vmem_limit_bytes=48 * 2**20),
        cost_estimate=pl.CostEstimate(
            flops=4 * rows * width * depth, bytes_accessed=26 * 2**20, transcendentals=0
        ),
    )(table, panel, statistic, noise, *pieces, *earlier)


def move(array, pairs):
    return lax.ppermute(array, AXES, pairs)


def shards(statistic, noise, grads):
    part = grads.shape[0] // STREAMS
    first = move(grads[:part], spread_pairs())
    first, rest = lax.optimization_barrier((first, grads))
    panel = lax.all_gather(rest, "col", axis=1, tiled=True)
    heads = [first, move(rest[part:], spread_pairs())]
    table = unit_table()
    total = None
    for stream, unit in enumerate(heads):
        own = jnp.stack([unit] + [move(unit, shift_pairs(i, True)) for i in (1, -1, 2)])
        ahead = move(own, shift_pairs(1, False))
        behind = move(own, shift_pairs(-1, False))
        low = move(ahead[:2], shift_pairs(1, False))
        high = move(behind[2:], shift_pairs(-1, False))
        total = blend(stream, table, panel, statistic, noise, [own, ahead, behind, low, high], total)
    return total


def solution(mesh):
    in_specs = (P("row", "col"), P("row", "col"), P("row", "col"))
    out_specs = P("row", "col")
    return jax.shard_map(shards, mesh=mesh, in_specs=in_specs, out_specs=out_specs, check_vma=False)
```

```python
import functools

import jax
import jax.numpy as jnp
from jax import lax
from jax.experimental import pallas as pl
from jax.experimental.pallas import tpu as pltpu
from jax.sharding import PartitionSpec as P

AXES = ("row", "col")
SIDE = 4
ORDER = (0, 1, 3, 2)
ROWS_TILE = 512
STREAMS = 2


def place(y, x, z, core):
    return (y % SIDE * SIDE + x % SIDE) * 2 * SIDE + z % SIDE * 2 + core


def coords():
    for y in range(SIDE):
        for x in range(SIDE):
            for z in range(SIDE):
                for core in range(2):
                    yield y, x, z, core


def turn(t):
    return t if t % 2 else (t + 2) % SIDE


def spread_pairs():
    pairs = []
    for y, x, z, core in coords():
        half = x // 2
        to_x = x if core == half else SIDE - 1 - x
        pairs.append((place(y, x, z, core), place(y + turn((z - y) % SIDE), to_x, y, half)))
    return pairs


def shift_pairs(step, first):
    pairs = []
    for y, x, z, core in coords():
        along_x = (core == 0) == first
        to = place(y, x - step, z, core) if along_x else place(y - step, x, z, core)
        pairs.append((place(y, x, z, core), to))
    return pairs


def unit_ids(offsets):
    row, col = lax.axis_index("row"), lax.axis_index("col")
    y, x, z, core = row // SIDE, row % SIDE, col // 2, col % 2
    blocks, eighths = [], []
    for j in offsets:
        for i in ORDER:
            uy = (y + jnp.where(core == 0, j, i)) % SIDE
            ux = (x + jnp.where(core == 0, i, j)) % SIDE
            t = (uy - z) % SIDE
            k = (z + jnp.where(t % 2 == 1, t, (t + 2) % SIDE)) % SIDE
            home = ux // 2 == core
            source_x = jnp.where(home, ux, SIDE - 1 - ux)
            blocks.append(source_x % 2)
            eighths.append(2 * k + jnp.where(home, core, 1 - core))
    return blocks, eighths, [row, col]


def tables(held):
    blocks, eighths, place_ids = held
    ones = sum(blocks)
    zeros = len(blocks) - ones
    slots, seen = [], jnp.int32(0)
    for n, block in enumerate(blocks):
        slots.append(jnp.where(block == 1, zeros + seen, n - seen))
        seen = seen + block
    return jnp.stack(slots + eighths + [zeros] + place_ids).astype(jnp.int32)


def blend_kernel(streams, pieces, fresh, table, panel, *refs):
    count = 1 + max(g for units in pieces for g, _ in units)
    groups, refs = refs[:count], refs[count:]
    carried, refs = refs[: 2 if fresh else 1], refs[2 if fresh else 1 :]
    out, left, right, tiles, added, lookup, left_sems, right_sems, in_sems, out_sems = refs[-10:]
    sources = [[groups[g].at[s] for g, s in units] for units in pieces]
    n = len(sources[0])
    eighths, rows, depth = left.shape
    width = right.shape[1]
    tile = tiles.shape[1]
    steps = [(m, q, b) for m in range(rows // tile) for q in range(len(streams)) for b in range(2)]

    def copy_right(q, u):
        slot = q * n + table[u]
        return pltpu.make_async_copy(sources[q][u], right.at[slot], right_sems.at[slot])

    def copy_left(s, m):
        eighth, span = s if fresh else table[n + s], pl.ds(m * tile, tile)
        return pltpu.make_async_copy(panel.at[eighth, span], left.at[s, span], left_sems.at[m, s])

    def window(ref, m, q, b):
        return ref.at[pl.ds(m * tile, tile), pl.ds((STREAMS * b + streams[q]) * width, width)]

    def copies_in(t):
        copies = [pltpu.make_async_copy(window(carried[0], *steps[t]), tiles.at[t], in_sems.at[0, t])]
        if fresh:
            copies.append(pltpu.make_async_copy(window(carried[1], *steps[t]), added.at[t], in_sems.at[1, t]))
        return copies

    def copy_out(t):
        return pltpu.make_async_copy(tiles.at[t], window(out, *steps[t]), out_sems.at[t])

    for s in range(eighths):
        copy_left(s, 0).start()
    for copy in copies_in(0):
        copy.start()
    for q in range(len(streams)):
        for u in range(n):
            copy_right(q, u).start()
    for t in range(1, len(steps)):
        if not fresh and steps[t][1:] == (0, 0):
            for s in range(eighths):
                copy_left(s, steps[t][0]).start()
        for copy in copies_in(t):
            copy.start()
    for u in range(n):
        lookup[table[u]] = table[n + u] if fresh else u

    zeros = table[2 * n]
    for t, (m, q, b) in enumerate(steps):
        first = q == 0 and b == 0
        if first:
            for s in range(eighths):
                copy_left(s, m).wait()
        for copy in copies_in(t):
            copy.wait()
        if fresh and first and m + 1 < rows // tile:
            for s in range(eighths):
                copy_left(s, m + 1).start()
        if fresh:
            tiles[t] = 0.9 * tiles[t] + 0.1 * added[t].astype(jnp.float32)

        def pair(p, _):
            if m == 0:
                for s in range(2):
                    slot = q * n + 2 * p + s
                    pltpu.make_async_copy(sources[0][0], right.at[slot], right_sems.at[slot]).wait()
            parts = [
                lax.dot_general(
                    left[lookup[2 * p + s], m * tile : (m + 1) * tile, :],
                    right[q * n + 2 * p + s],
                    (((1,), (1,)), ((), ())),
                    preferred_element_type=jnp.float32,
                )
                for s in range(2)
            ]
            tiles[t] += 0.1 * (parts[0] + parts[1])
            return 0

        lax.fori_loop(0 if b == 0 else zeros // 2, zeros // 2 if b == 0 else n // 2, pair, 0)
        at_row = table[2 * n + 1] * rows + m * tile + lax.broadcasted_iota(jnp.int32, (tile, width), 0)
        at_col = (table[2 * n + 2] * 2 + b) * (width * STREAMS) + streams[q] * width
        at_col = at_col + lax.broadcasted_iota(jnp.int32, (tile, width), 1)
        tiles[t] = jnp.where(at_row >= at_col, tiles[t], 0.0)
        copy_out(t).start()
    for t in range(len(steps)):
        copy_out(t).wait()


def blend(streams, pieces, table, panel, groups, fresh, before):
    eighths, rows, depth = panel.shape
    n, width = len(pieces[0]), groups[0].shape[1]
    held = n if fresh is None else eighths
    count = 2 * len(streams) * rows // ROWS_TILE
    carried = [before] if fresh is None else list(fresh)
    extra = [] if fresh is None or before is None else [before]
    operands = [table, panel, *groups, *carried, *extra]
    anywhere = pl.BlockSpec(memory_space=pl.ANY)
    return pl.pallas_call(
        functools.partial(blend_kernel, streams, pieces, fresh is not None),
        in_specs=[pl.BlockSpec(memory_space=pltpu.SMEM)] + [anywhere] * (len(operands) - 1),
        out_specs=anywhere,
        scratch_shapes=[
            pltpu.VMEM((held, rows, depth), jnp.bfloat16),
            pltpu.VMEM((len(streams) * n, width, depth), jnp.bfloat16),
            pltpu.VMEM((count, ROWS_TILE, width), jnp.float32),
            pltpu.VMEM((count if fresh else 1, ROWS_TILE, width), jnp.bfloat16),
            pltpu.SMEM((n,), jnp.int32),
            pltpu.SemaphoreType.DMA((rows // ROWS_TILE, held)),
            pltpu.SemaphoreType.DMA((len(streams) * n,)),
            pltpu.SemaphoreType.DMA((2, count)),
            pltpu.SemaphoreType.DMA((count,)),
        ],
        out_shape=jax.ShapeDtypeStruct((rows, 2 * STREAMS * width), jnp.float32),
        input_output_aliases={} if before is None else {len(operands) - 1: 0},
        compiler_params=pltpu.CompilerParams(vmem_limit_bytes=58 * 2**20),
        cost_estimate=pl.CostEstimate(
            flops=2 * len(streams) * n * rows * width * depth, bytes_accessed=24 * 2**20, transcendentals=0
        ),
    )(*operands)


def move(array, pairs):
    return lax.ppermute(array, AXES, pairs)


def shards(statistic, noise, grads):
    part = grads.shape[0] // STREAMS
    first = move(grads[:part], spread_pairs())
    first, rest = lax.optimization_barrier((first, grads))
    panel = lax.all_gather(rest, "col", axis=0)
    heads = [first, move(rest[part:], spread_pairs())]
    near, far = tables(unit_ids((0, 1, 3))), tables(unit_ids((2,)))
    inputs = (statistic, noise)

    def gather(unit):
        own = jnp.stack([unit] + [move(unit, shift_pairs(i, True)) for i in (1, -1, 2)])
        return own, move(own, shift_pairs(1, False)), move(own, shift_pairs(-1, False))

    def forward(ahead, behind):
        return move(ahead[:2], shift_pairs(1, False)), move(behind[2:], shift_pairs(-1, False))

    held = [gather(unit) for unit in heads]
    units = [tuple((g, s) for g in range(3) for s in range(SIDE))]
    distant = forward(*held[0][1:])
    total = blend((0,), units, near, panel, held[0], inputs, None)
    (own, ahead, behind), total = lax.optimization_barrier((held[1], total))
    distant += forward(ahead, behind)
    total = blend((1,), units, near, panel, (own, ahead, behind), inputs, total)
    units = [tuple((2 * q + g, s) for g in range(2) for s in range(2)) for q in range(STREAMS)]
    return blend((0, 1), units, far, panel, distant, None, total)


def solution(mesh):
    in_specs = (P("row", "col"), P("row", "col"), P("row", "col"))
    out_specs = P("row", "col")
    return jax.shard_map(shards, mesh=mesh, in_specs=in_specs, out_specs=out_specs, check_vma=False)
```

```python
import functools

import jax
import jax.numpy as jnp
from jax import lax
from jax.experimental import pallas as pl
from jax.experimental.pallas import tpu as pltpu
from jax.sharding import PartitionSpec as P

AXES = ("row", "col")
SIDE = 4
ORDER = (0, 1, 3, 2)
ROWS_TILE = 512
STREAMS = 2


def place(y, x, z, core):
    return (y % SIDE * SIDE + x % SIDE) * 2 * SIDE + z % SIDE * 2 + core


def coords():
    for y in range(SIDE):
        for x in range(SIDE):
            for z in range(SIDE):
                for core in range(2):
                    yield y, x, z, core


def turn(t):
    return t if t % 2 else (t + 2) % SIDE


def spread_pairs():
    pairs = []
    for y, x, z, core in coords():
        half = x // 2
        to_x = x if core == half else SIDE - 1 - x
        pairs.append((place(y, x, z, core), place(y + turn((z - y) % SIDE), to_x, y, half)))
    return pairs


def shift_pairs(step, first):
    pairs = []
    for y, x, z, core in coords():
        along_x = (core == 0) == first
        to = place(y, x - step, z, core) if along_x else place(y - step, x, z, core)
        pairs.append((place(y, x, z, core), to))
    return pairs


def unit_ids(offsets):
    row, col = lax.axis_index("row"), lax.axis_index("col")
    y, x, z, core = row // SIDE, row % SIDE, col // 2, col % 2
    blocks, eighths = [], []
    for j in offsets:
        for i in ORDER:
            uy = (y + jnp.where(core == 0, j, i)) % SIDE
            ux = (x + jnp.where(core == 0, i, j)) % SIDE
            t = (uy - z) % SIDE
            k = (z + jnp.where(t % 2 == 1, t, (t + 2) % SIDE)) % SIDE
            home = ux // 2 == core
            source_x = jnp.where(home, ux, SIDE - 1 - ux)
            blocks.append(source_x % 2)
            eighths.append(2 * k + jnp.where(home, core, 1 - core))
    return blocks, eighths, [row, col]


def tables(held):
    blocks, eighths, place_ids = held
    ones = sum(blocks)
    zeros = len(blocks) - ones
    slots, seen = [], jnp.int32(0)
    for n, block in enumerate(blocks):
        slots.append(jnp.where(block == 1, zeros + seen, n - seen))
        seen = seen + block
    return jnp.stack(slots + eighths + [zeros] + place_ids).astype(jnp.int32)


def blend_kernel(streams, pieces, fresh, table, panel, *refs):
    count = 1 + max(g for units in pieces for g, _ in units)
    groups, refs = refs[:count], refs[count:]
    carried, refs = refs[: 2 if fresh else 1], refs[2 if fresh else 1 :]
    out, left, right, tiles, added, lookup, left_sems, right_sems, in_sems, out_sems = refs[-10:]
    sources = [[groups[g].at[s] for g, s in units] for units in pieces]
    n = len(sources[0])
    eighths, rows, depth = left.shape
    width = right.shape[1]
    tile = tiles.shape[1]
    steps = [(m, q, b) for m in range(rows // tile) for q in range(len(streams)) for b in range(2)]

    def copy_right(q, u):
        slot = q * n + table[u]
        return pltpu.make_async_copy(sources[q][u], right.at[slot], right_sems.at[slot])

    def copy_left(s, m):
        eighth, span = s if fresh else table[n + s], pl.ds(m * tile, tile)
        return pltpu.make_async_copy(panel.at[eighth, span], left.at[s, span], left_sems.at[m, s])

    def window(ref, m, q, b):
        return ref.at[pl.ds(m * tile, tile), pl.ds((STREAMS * b + streams[q]) * width, width)]

    def copies_in(t):
        copies = [pltpu.make_async_copy(window(carried[0], *steps[t]), tiles.at[t], in_sems.at[0, t])]
        if fresh:
            copies.append(pltpu.make_async_copy(window(carried[1], *steps[t]), added.at[t], in_sems.at[1, t]))
        return copies

    def copy_out(t):
        return pltpu.make_async_copy(tiles.at[t], window(out, *steps[t]), out_sems.at[t])

    for s in range(eighths):
        copy_left(s, 0).start()
    lead = 1 if fresh else 3
    for t in range(lead):
        for copy in copies_in(t):
            copy.start()
    for q in range(len(streams)):
        for u in range(n):
            copy_right(q, u).start()
    for u in range(n):
        lookup[table[u]] = table[n + u] if fresh else u

    zeros = table[2 * n]
    for t, (m, q, b) in enumerate(steps):
        first = q == 0 and b == 0
        if first:
            for s in range(eighths):
                copy_left(s, m).wait()
        for copy in copies_in(t):
            copy.wait()
        if first and m + 1 < rows // tile:
            for s in range(eighths):
                copy_left(s, m + 1).start()
        if t + lead < len(steps):
            for copy in copies_in(t + lead):
                copy.start()
        if fresh:
            tiles[t] = 0.9 * tiles[t] + 0.1 * added[t].astype(jnp.float32)

        def pair(p, _):
            if m == 0:
                for s in range(2):
                    slot = q * n + 2 * p + s
                    pltpu.make_async_copy(sources[0][0], right.at[slot], right_sems.at[slot]).wait()
            parts = [
                lax.dot_general(
                    left[lookup[2 * p + s], m * tile : (m + 1) * tile, :],
                    right[q * n + 2 * p + s],
                    (((1,), (1,)), ((), ())),
                    preferred_element_type=jnp.float32,
                )
                for s in range(2)
            ]
            tiles[t] += 0.1 * (parts[0] + parts[1])
            return 0

        lax.fori_loop(0 if b == 0 else zeros // 2, zeros // 2 if b == 0 else n // 2, pair, 0)
        top = table[2 * n + 1] * rows + m * tile
        side = (table[2 * n + 2] * 2 + b) * (width * STREAMS) + streams[q] * width

        @pl.when(top < side + width - 1)
        def _():
            at_row = top + lax.broadcasted_iota(jnp.int32, (tile, width), 0)
            at_col = side + lax.broadcasted_iota(jnp.int32, (tile, width), 1)
            tiles[t] = jnp.where(at_row >= at_col, tiles[t], 0.0)

        copy_out(t).start()
    for t in range(len(steps)):
        copy_out(t).wait()


def blend(streams, pieces, table, panel, groups, fresh, before):
    eighths, rows, depth = panel.shape
    n, width = len(pieces[0]), groups[0].shape[1]
    held = n if fresh is None else eighths
    count = 2 * len(streams) * rows // ROWS_TILE
    carried = [before] if fresh is None else list(fresh)
    extra = [] if fresh is None or before is None else [before]
    operands = [table, panel, *groups, *carried, *extra]
    anywhere = pl.BlockSpec(memory_space=pl.ANY)
    return pl.pallas_call(
        functools.partial(blend_kernel, streams, pieces, fresh is not None),
        in_specs=[pl.BlockSpec(memory_space=pltpu.SMEM)] + [anywhere] * (len(operands) - 1),
        out_specs=anywhere,
        scratch_shapes=[
            pltpu.VMEM((held, rows, depth), jnp.bfloat16),
            pltpu.VMEM((len(streams) * n, width, depth), jnp.bfloat16),
            pltpu.VMEM((count, ROWS_TILE, width), jnp.float32),
            pltpu.VMEM((count if fresh else 1, ROWS_TILE, width), jnp.bfloat16),
            pltpu.SMEM((n,), jnp.int32),
            pltpu.SemaphoreType.DMA((rows // ROWS_TILE, held)),
            pltpu.SemaphoreType.DMA((len(streams) * n,)),
            pltpu.SemaphoreType.DMA((2, count)),
            pltpu.SemaphoreType.DMA((count,)),
        ],
        out_shape=jax.ShapeDtypeStruct((rows, 2 * STREAMS * width), jnp.float32),
        input_output_aliases={} if before is None else {len(operands) - 1: 0},
        compiler_params=pltpu.CompilerParams(vmem_limit_bytes=58 * 2**20),
        cost_estimate=pl.CostEstimate(
            flops=2 * len(streams) * n * rows * width * depth, bytes_accessed=24 * 2**20, transcendentals=0
        ),
    )(*operands)


def move(array, pairs):
    return lax.ppermute(array, AXES, pairs)


def shards(statistic, noise, grads):
    part = grads.shape[0] // STREAMS
    first = move(grads[:part], spread_pairs())
    first, rest = lax.optimization_barrier((first, grads))
    panel = lax.all_gather(rest, "col", axis=0)
    heads = [first, move(rest[part:], spread_pairs())]
    near, far = tables(unit_ids((0, 1, 3))), tables(unit_ids((2,)))
    inputs = (statistic, noise)

    def gather(unit):
        own = jnp.stack([unit] + [move(unit, shift_pairs(i, True)) for i in (1, -1, 2)])
        return own, move(own, shift_pairs(1, False)), move(own, shift_pairs(-1, False))

    held = [gather(unit) for unit in heads]
    units = [tuple((g, s) for g in range(3) for s in range(SIDE))]
    distant = [move(held[0][1], shift_pairs(1, False))]
    total = blend((0,), units, near, panel, held[0], inputs, None)
    (own, ahead, behind), total = lax.optimization_barrier((held[1], total))
    distant += [move(ahead[:2], shift_pairs(1, False)), move(behind[2:], shift_pairs(-1, False))]
    total = blend((1,), units, near, panel, (own, ahead, behind), inputs, total)
    units = [tuple((0, s) for s in range(SIDE)), tuple((1 + g, s) for g in range(2) for s in range(2))]
    return blend((0, 1), units, far, panel, distant, None, total)


def solution(mesh):
    in_specs = (P("row", "col"), P("row", "col"), P("row", "col"))
    out_specs = P("row", "col")
    return jax.shard_map(shards, mesh=mesh, in_specs=in_specs, out_specs=out_specs, check_vma=False)
```

```python
import functools

import jax
import jax.numpy as jnp
from jax import lax
from jax.experimental import pallas as pl
from jax.experimental.pallas import tpu as pltpu
from jax.sharding import PartitionSpec as P

AXES = ("row", "col")
SIDE = 4
ORDER = (0, 1, 3, 2)
ROWS_TILE = 512
STREAMS = 2


def place(y, x, z, core):
    return (y % SIDE * SIDE + x % SIDE) * 2 * SIDE + z % SIDE * 2 + core


def coords():
    for y in range(SIDE):
        for x in range(SIDE):
            for z in range(SIDE):
                for core in range(2):
                    yield y, x, z, core


def turn(t):
    return t if t % 2 else (t + 2) % SIDE


def spread_pairs():
    pairs = []
    for y, x, z, core in coords():
        half = x // 2
        to_x = x if core == half else SIDE - 1 - x
        pairs.append((place(y, x, z, core), place(y + turn((z - y) % SIDE), to_x, y, half)))
    return pairs


def shift_pairs(step, first):
    pairs = []
    for y, x, z, core in coords():
        along_x = (core == 0) == first
        to = place(y, x - step, z, core) if along_x else place(y - step, x, z, core)
        pairs.append((place(y, x, z, core), to))
    return pairs


def unit_ids(offsets):
    row, col = lax.axis_index("row"), lax.axis_index("col")
    y, x, z, core = row // SIDE, row % SIDE, col // 2, col % 2
    blocks, eighths = [], []
    for j in offsets:
        for i in ORDER:
            uy = (y + jnp.where(core == 0, j, i)) % SIDE
            ux = (x + jnp.where(core == 0, i, j)) % SIDE
            t = (uy - z) % SIDE
            k = (z + jnp.where(t % 2 == 1, t, (t + 2) % SIDE)) % SIDE
            home = ux // 2 == core
            source_x = jnp.where(home, ux, SIDE - 1 - ux)
            blocks.append(source_x % 2)
            eighths.append(2 * k + jnp.where(home, core, 1 - core))
    return blocks, eighths, [row, col]


def tables(held):
    blocks, eighths, place_ids = held
    ones = sum(blocks)
    zeros = len(blocks) - ones
    slots, seen = [], jnp.int32(0)
    for n, block in enumerate(blocks):
        slots.append(jnp.where(block == 1, zeros + seen, n - seen))
        seen = seen + block
    return jnp.stack(slots + eighths + [zeros] + place_ids).astype(jnp.int32)


def blend_kernel(streams, pieces, fresh, table, panel, *refs):
    count = 1 + max(g for units in pieces for g, _ in units)
    groups, refs = refs[:count], refs[count:]
    carried, refs = refs[: 2 if fresh else 1], refs[2 if fresh else 1 :]
    out, left, right, tiles, added, lookup, left_sems, right_sems, in_sems, out_sems = refs[-10:]
    sources = [[groups[g].at[s] for g, s in units] for units in pieces]
    n = len(sources[0])
    eighths, rows, depth = left.shape
    width = right.shape[1]
    tile = tiles.shape[1]
    steps = [(m, q, b) for m in range(rows // tile) for q in range(len(streams)) for b in range(2)]

    def copy_right(q, u):
        slot = q * n + table[u]
        return pltpu.make_async_copy(sources[q][u], right.at[slot], right_sems.at[slot])

    def copy_left(s, m):
        eighth, span = s if fresh else table[n + s], pl.ds(m * tile, tile)
        return pltpu.make_async_copy(panel.at[eighth, span], left.at[s, span], left_sems.at[m, s])

    def window(ref, m, q, b):
        return ref.at[pl.ds(m * tile, tile), pl.ds((STREAMS * b + streams[q]) * width, width)]

    def copies_in(t):
        copies = [pltpu.make_async_copy(window(carried[0], *steps[t]), tiles.at[t], in_sems.at[0, t])]
        if fresh:
            copies.append(pltpu.make_async_copy(window(carried[1], *steps[t]), added.at[t], in_sems.at[1, t]))
        return copies

    def copy_out(t):
        return pltpu.make_async_copy(tiles.at[t], window(out, *steps[t]), out_sems.at[t])

    for s in range(eighths):
        copy_left(s, 0).start()
    lead = 1 if fresh else 3
    for t in range(lead):
        for copy in copies_in(t):
            copy.start()
    for q in range(len(streams)):
        for u in range(n):
            copy_right(q, u).start()
    for u in range(n):
        lookup[table[u]] = table[n + u] if fresh else u

    zeros = table[2 * n]
    for t, (m, q, b) in enumerate(steps):
        first = q == 0 and b == 0
        if first:
            for s in range(eighths):
                copy_left(s, m).wait()
        for copy in copies_in(t):
            copy.wait()
        if first and m + 1 < rows // tile:
            for s in range(eighths):
                copy_left(s, m + 1).start()
        if t + lead < len(steps):
            for copy in copies_in(t + lead):
                copy.start()
        if fresh:
            tiles[t] = 0.9 * tiles[t] + 0.1 * added[t].astype(jnp.float32)

        def pair(p, _):
            if m == 0:
                for s in range(2):
                    slot = q * n + 2 * p + s
                    pltpu.make_async_copy(sources[0][0], right.at[slot], right_sems.at[slot]).wait()
            parts = [
                lax.dot_general(
                    left[lookup[2 * p + s], m * tile : (m + 1) * tile, :],
                    right[q * n + 2 * p + s],
                    (((1,), (1,)), ((), ())),
                    preferred_element_type=jnp.float32,
                )
                for s in range(2)
            ]
            tiles[t] += 0.1 * (parts[0] + parts[1])
            return 0

        lax.fori_loop(0 if b == 0 else zeros // 2, zeros // 2 if b == 0 else n // 2, pair, 0)
        top = table[2 * n + 1] * rows + m * tile
        side = (table[2 * n + 2] * 2 + b) * (width * STREAMS) + streams[q] * width

        @pl.when(top < side + width - 1)
        def _():
            at_row = top + lax.broadcasted_iota(jnp.int32, (tile, width), 0)
            at_col = side + lax.broadcasted_iota(jnp.int32, (tile, width), 1)
            tiles[t] = jnp.where(at_row >= at_col, tiles[t], 0.0)

        copy_out(t).start()
    for t in range(len(steps)):
        copy_out(t).wait()


def blend(streams, pieces, table, panel, groups, fresh, before):
    eighths, rows, depth = panel.shape
    n, width = len(pieces[0]), groups[0].shape[1]
    held = n if fresh is None else eighths
    count = 2 * len(streams) * rows // ROWS_TILE
    carried = [before] if fresh is None else list(fresh)
    extra = [] if fresh is None or before is None else [before]
    operands = [table, panel, *groups, *carried, *extra]
    anywhere = pl.BlockSpec(memory_space=pl.ANY)
    return pl.pallas_call(
        functools.partial(blend_kernel, streams, pieces, fresh is not None),
        in_specs=[pl.BlockSpec(memory_space=pltpu.SMEM)] + [anywhere] * (len(operands) - 1),
        out_specs=anywhere,
        scratch_shapes=[
            pltpu.VMEM((held, rows, depth), jnp.bfloat16),
            pltpu.VMEM((len(streams) * n, width, depth), jnp.bfloat16),
            pltpu.VMEM((count, ROWS_TILE, width), jnp.float32),
            pltpu.VMEM((count if fresh else 1, ROWS_TILE, width), jnp.bfloat16),
            pltpu.SMEM((n,), jnp.int32),
            pltpu.SemaphoreType.DMA((rows // ROWS_TILE, held)),
            pltpu.SemaphoreType.DMA((len(streams) * n,)),
            pltpu.SemaphoreType.DMA((2, count)),
            pltpu.SemaphoreType.DMA((count,)),
        ],
        out_shape=jax.ShapeDtypeStruct((rows, 2 * STREAMS * width), jnp.float32),
        input_output_aliases={} if before is None else {len(operands) - 1: 0},
        compiler_params=pltpu.CompilerParams(vmem_limit_bytes=58 * 2**20),
        cost_estimate=pl.CostEstimate(
            flops=2 * len(streams) * n * rows * width * depth, bytes_accessed=24 * 2**20, transcendentals=0
        ),
    )(*operands)


def move(array, pairs):
    return lax.ppermute(array, AXES, pairs)


def shards(statistic, noise, grads):
    part = grads.shape[0] // STREAMS
    first = move(grads[:part], spread_pairs())
    first, rest = lax.optimization_barrier((first, grads))
    panel = lax.all_gather(rest, "col", axis=0)
    heads = [first, move(rest[part:], spread_pairs())]
    near, far = tables(unit_ids((0, 1, 3))), tables(unit_ids((2,)))
    inputs = (statistic, noise)

    def gather(unit):
        own = jnp.stack([unit] + [move(unit, shift_pairs(i, True)) for i in (1, -1, 2)])
        return own, move(own, shift_pairs(1, False)), move(own, shift_pairs(-1, False))

    def forward(ahead, behind):
        return move(ahead[:2], shift_pairs(1, False)), move(behind[2:], shift_pairs(-1, False))

    held = [gather(unit) for unit in heads]
    units = [tuple((g, s) for g in range(3) for s in range(SIDE))]
    distant = forward(*held[0][1:])
    total = blend((0,), units, near, panel, held[0], inputs, None)
    (own, ahead, behind), total = lax.optimization_barrier((held[1], total))
    distant += forward(ahead, behind)
    total = blend((1,), units, near, panel, (own, ahead, behind), inputs, total)
    units = [tuple((2 * q + g, s) for g in range(2) for s in range(2)) for q in range(STREAMS)]
    return blend((0, 1), units, far, panel, distant, None, total)


def solution(mesh):
    in_specs = (P("row", "col"), P("row", "col"), P("row", "col"))
    out_specs = P("row", "col")
    return jax.shard_map(shards, mesh=mesh, in_specs=in_specs, out_specs=out_specs, check_vma=False)
```

```python
import functools

import jax
import jax.numpy as jnp
from jax import lax
from jax.experimental import pallas as pl
from jax.experimental.pallas import tpu as pltpu
from jax.sharding import PartitionSpec as P

AXES = ("row", "col")
SIDE = 4
ORDER = (0, 1, 3, 2)
ROWS_TILE = 512
STREAMS = 2


def place(y, x, z, core):
    return (y % SIDE * SIDE + x % SIDE) * 2 * SIDE + z % SIDE * 2 + core


def coords():
    for y in range(SIDE):
        for x in range(SIDE):
            for z in range(SIDE):
                for core in range(2):
                    yield y, x, z, core


def turn(t):
    return t if t % 2 else (t + 2) % SIDE


def spread_pairs():
    pairs = []
    for y, x, z, core in coords():
        half = x // 2
        to_x = x if core == half else SIDE - 1 - x
        pairs.append((place(y, x, z, core), place(y + turn((z - y) % SIDE), to_x, y, half)))
    return pairs


def shift_pairs(step, first):
    pairs = []
    for y, x, z, core in coords():
        along_x = (core == 0) == first
        to = place(y, x - step, z, core) if along_x else place(y - step, x, z, core)
        pairs.append((place(y, x, z, core), to))
    return pairs


def unit_ids(offsets):
    row, col = lax.axis_index("row"), lax.axis_index("col")
    y, x, z, core = row // SIDE, row % SIDE, col // 2, col % 2
    blocks, eighths = [], []
    for j in offsets:
        for i in ORDER:
            uy = (y + jnp.where(core == 0, j, i)) % SIDE
            ux = (x + jnp.where(core == 0, i, j)) % SIDE
            t = (uy - z) % SIDE
            k = (z + jnp.where(t % 2 == 1, t, (t + 2) % SIDE)) % SIDE
            home = ux // 2 == core
            source_x = jnp.where(home, ux, SIDE - 1 - ux)
            blocks.append(source_x % 2)
            eighths.append(2 * k + jnp.where(home, core, 1 - core))
    return blocks, eighths, [row, col]


def tables(held):
    blocks, eighths, place_ids = held
    ones = sum(blocks)
    zeros = len(blocks) - ones
    slots, seen = [], jnp.int32(0)
    for n, block in enumerate(blocks):
        slots.append(jnp.where(block == 1, zeros + seen, n - seen))
        seen = seen + block
    return jnp.stack(slots + eighths + [zeros] + place_ids).astype(jnp.int32)


def blend_kernel(streams, pieces, fresh, table, panel, *refs):
    count = 1 + max(g for units in pieces for g, _ in units)
    groups, refs = refs[:count], refs[count:]
    carried, refs = refs[: 2 if fresh else 1], refs[2 if fresh else 1 :]
    out, left, right, tiles, added, lookup, left_sems, right_sems, in_sems, out_sems = refs[-10:]
    sources = [[groups[g].at[s] for g, s in units] for units in pieces]
    n = len(sources[0])
    eighths, rows, depth = left.shape
    width = right.shape[1]
    tile = tiles.shape[1]
    steps = [(m, q, b) for m in range(rows // tile) for q in range(len(streams)) for b in range(2)]

    def copy_right(q, u):
        slot = q * n + table[u]
        return pltpu.make_async_copy(sources[q][u], right.at[slot], right_sems.at[slot])

    def copy_left(s, m):
        eighth, span = s if fresh else table[n + s], pl.ds(m * tile, tile)
        return pltpu.make_async_copy(panel.at[eighth, span], left.at[s, span], left_sems.at[m, s])

    def window(ref, m, q, b):
        return ref.at[pl.ds(m * tile, tile), pl.ds((STREAMS * b + streams[q]) * width, width)]

    def copies_in(t):
        copies = [pltpu.make_async_copy(window(carried[0], *steps[t]), tiles.at[t], in_sems.at[0, t])]
        if fresh:
            copies.append(pltpu.make_async_copy(window(carried[1], *steps[t]), added.at[t], in_sems.at[1, t]))
        return copies

    def copy_out(t):
        return pltpu.make_async_copy(tiles.at[t], window(out, *steps[t]), out_sems.at[t])

    for s in range(eighths):
        copy_left(s, 0).start()
    lead = 1 if fresh else 3
    for t in range(lead):
        for copy in copies_in(t):
            copy.start()
    for q in range(len(streams)):
        for u in range(n):
            copy_right(q, u).start()
    for u in range(n):
        lookup[table[u]] = table[n + u] if fresh else u

    zeros = table[2 * n]
    for t, (m, q, b) in enumerate(steps):
        first = q == 0 and b == 0
        if first:
            for s in range(eighths):
                copy_left(s, m).wait()
        for copy in copies_in(t):
            copy.wait()
        if first and m + 1 < rows // tile:
            for s in range(eighths):
                copy_left(s, m + 1).start()
        if t + lead < len(steps):
            for copy in copies_in(t + lead):
                copy.start()
        if fresh:
            tiles[t] = 0.9 * tiles[t] + 0.1 * added[t].astype(jnp.float32)

        def pair(p, _):
            if m == 0:
                for s in range(2):
                    slot = q * n + 2 * p + s
                    pltpu.make_async_copy(sources[0][0], right.at[slot], right_sems.at[slot]).wait()
            parts = [
                lax.dot_general(
                    left[lookup[2 * p + s], m * tile : (m + 1) * tile, :],
                    right[q * n + 2 * p + s],
                    (((1,), (1,)), ((), ())),
                    preferred_element_type=jnp.float32,
                )
                for s in range(2)
            ]
            tiles[t] += 0.1 * (parts[0] + parts[1])
            return 0

        lax.fori_loop(0 if b == 0 else zeros // 2, zeros // 2 if b == 0 else n // 2, pair, 0)
        top = table[2 * n + 1] * rows + m * tile
        side = (table[2 * n + 2] * 2 + b) * (width * STREAMS) + streams[q] * width

        @pl.when(top < side + width - 1)
        def _():
            at_row = top + lax.broadcasted_iota(jnp.int32, (tile, width), 0)
            at_col = side + lax.broadcasted_iota(jnp.int32, (tile, width), 1)
            tiles[t] = jnp.where(at_row >= at_col, tiles[t], 0.0)

        copy_out(t).start()
    for t in range(len(steps)):
        copy_out(t).wait()


def blend(streams, pieces, table, panel, groups, fresh, before):
    eighths, rows, depth = panel.shape
    n, width = len(pieces[0]), groups[0].shape[1]
    held = n if fresh is None else eighths
    count = 2 * len(streams) * rows // ROWS_TILE
    carried = [before] if fresh is None else list(fresh)
    extra = [] if fresh is None or before is None else [before]
    operands = [table, panel, *groups, *carried, *extra]
    anywhere = pl.BlockSpec(memory_space=pl.ANY)
    return pl.pallas_call(
        functools.partial(blend_kernel, streams, pieces, fresh is not None),
        in_specs=[pl.BlockSpec(memory_space=pltpu.SMEM)] + [anywhere] * (len(operands) - 1),
        out_specs=anywhere,
        scratch_shapes=[
            pltpu.VMEM((held, rows, depth), jnp.bfloat16),
            pltpu.VMEM((len(streams) * n, width, depth), jnp.bfloat16),
            pltpu.VMEM((count, ROWS_TILE, width), jnp.float32),
            pltpu.VMEM((count if fresh else 1, ROWS_TILE, width), jnp.bfloat16),
            pltpu.SMEM((n,), jnp.int32),
            pltpu.SemaphoreType.DMA((rows // ROWS_TILE, held)),
            pltpu.SemaphoreType.DMA((len(streams) * n,)),
            pltpu.SemaphoreType.DMA((2, count)),
            pltpu.SemaphoreType.DMA((count,)),
        ],
        out_shape=jax.ShapeDtypeStruct((rows, 2 * STREAMS * width), jnp.float32),
        input_output_aliases={} if before is None else {len(operands) - 1: 0},
        compiler_params=pltpu.CompilerParams(vmem_limit_bytes=58 * 2**20),
        cost_estimate=pl.CostEstimate(
            flops=2 * len(streams) * n * rows * width * depth, bytes_accessed=24 * 2**20, transcendentals=0
        ),
    )(*operands)


def halves_kernel(ahead, behind, low, high, sems):
    count = low.shape[0]
    copies = [pltpu.make_async_copy(ahead.at[s], low.at[s], sems.at[0, s]) for s in range(count)]
    copies += [pltpu.make_async_copy(behind.at[count + s], high.at[s], sems.at[1, s]) for s in range(count)]
    for copy in copies:
        copy.start()
    for copy in copies:
        copy.wait()


def halves(ahead, behind):
    count, width, depth = ahead.shape
    half = jax.ShapeDtypeStruct((count // 2, width, depth), ahead.dtype)
    anywhere = pl.BlockSpec(memory_space=pl.ANY)
    return pl.pallas_call(
        halves_kernel,
        in_specs=[anywhere, anywhere],
        out_specs=[anywhere, anywhere],
        out_shape=[half, half],
        scratch_shapes=[pltpu.SemaphoreType.DMA((2, count // 2))],
        compiler_params=pltpu.CompilerParams(vmem_limit_bytes=58 * 2**20),
        cost_estimate=pl.CostEstimate(flops=0, bytes_accessed=4 * 2**20, transcendentals=0),
    )(ahead, behind)


def move(array, pairs):
    return lax.ppermute(array, AXES, pairs)


def shards(statistic, noise, grads):
    part = grads.shape[0] // STREAMS
    first = move(grads[:part], spread_pairs())
    first, rest = lax.optimization_barrier((first, grads))
    panel = lax.all_gather(rest, "col", axis=0)
    heads = [first, move(rest[part:], spread_pairs())]
    near, far = tables(unit_ids((0, 1, 3))), tables(unit_ids((2,)))
    inputs = (statistic, noise)

    def gather(unit):
        own = jnp.stack([unit] + [move(unit, shift_pairs(i, True)) for i in (1, -1, 2)])
        return own, move(own, shift_pairs(1, False)), move(own, shift_pairs(-1, False))

    def forward(ahead, behind):
        low, high = halves(ahead, behind)
        return move(low, shift_pairs(1, False)), move(high, shift_pairs(-1, False))

    held = [gather(unit) for unit in heads]
    units = [tuple((g, s) for g in range(3) for s in range(SIDE))]
    distant = forward(*held[0][1:])
    total = blend((0,), units, near, panel, held[0], inputs, None)
    (own, ahead, behind), total = lax.optimization_barrier((held[1], total))
    distant += forward(ahead, behind)
    total = blend((1,), units, near, panel, (own, ahead, behind), inputs, total)
    units = [tuple((2 * q + g, s) for g in range(2) for s in range(2)) for q in range(STREAMS)]
    return blend((0, 1), units, far, panel, distant, None, total)


def solution(mesh):
    in_specs = (P("row", "col"), P("row", "col"), P("row", "col"))
    out_specs = P("row", "col")
    return jax.shard_map(shards, mesh=mesh, in_specs=in_specs, out_specs=out_specs, check_vma=False)
```

```python
import functools

import jax
import jax.numpy as jnp
from jax import lax
from jax.experimental import pallas as pl
from jax.experimental.pallas import tpu as pltpu
from jax.sharding import PartitionSpec as P

AXES = ("row", "col")
SIDE = 4
ORDER = (0, 1, 3, 2)
ROWS_TILE = 512
STREAMS = 2


def place(y, x, z, core):
    return (y % SIDE * SIDE + x % SIDE) * 2 * SIDE + z % SIDE * 2 + core


def coords():
    for y in range(SIDE):
        for x in range(SIDE):
            for z in range(SIDE):
                for core in range(2):
                    yield y, x, z, core


def turn(t):
    return t if t % 2 else (t + 2) % SIDE


def spread_pairs():
    pairs = []
    for y, x, z, core in coords():
        half = x // 2
        to_x = x if core == half else SIDE - 1 - x
        pairs.append((place(y, x, z, core), place(y + turn((z - y) % SIDE), to_x, y, half)))
    return pairs


def shift_pairs(step, first):
    pairs = []
    for y, x, z, core in coords():
        along_x = (core == 0) == first
        to = place(y, x - step, z, core) if along_x else place(y - step, x, z, core)
        pairs.append((place(y, x, z, core), to))
    return pairs


def unit_ids(offsets):
    row, col = lax.axis_index("row"), lax.axis_index("col")
    y, x, z, core = row // SIDE, row % SIDE, col // 2, col % 2
    blocks, eighths = [], []
    for j in offsets:
        for i in ORDER:
            uy = (y + jnp.where(core == 0, j, i)) % SIDE
            ux = (x + jnp.where(core == 0, i, j)) % SIDE
            t = (uy - z) % SIDE
            k = (z + jnp.where(t % 2 == 1, t, (t + 2) % SIDE)) % SIDE
            home = ux // 2 == core
            source_x = jnp.where(home, ux, SIDE - 1 - ux)
            blocks.append(source_x % 2)
            eighths.append(2 * k + jnp.where(home, core, 1 - core))
    return blocks, eighths, [row, col]


def tables(held):
    blocks, eighths, place_ids = held
    ones = sum(blocks)
    zeros = len(blocks) - ones
    slots, seen = [], jnp.int32(0)
    for n, block in enumerate(blocks):
        slots.append(jnp.where(block == 1, zeros + seen, n - seen))
        seen = seen + block
    return jnp.stack(slots + eighths + [zeros] + place_ids).astype(jnp.int32)


def blend_kernel(streams, pieces, fresh, table, panel, *refs):
    count = 1 + max(g for units in pieces for g, _ in units)
    groups, refs = refs[:count], refs[count:]
    carried, refs = refs[: 2 if fresh else 1], refs[2 if fresh else 1 :]
    out, left, right, tiles, added, lookup, left_sems, right_sems, in_sems, out_sems = refs[-10:]
    sources = [[groups[g].at[s] for g, s in units] for units in pieces]
    n = len(sources[0])
    eighths, rows, depth = left.shape
    width = right.shape[1]
    tile = tiles.shape[1]
    steps = [(m, q, b) for m in range(rows // tile) for q in range(len(streams)) for b in range(2)]

    def copy_right(q, u):
        slot = q * n + table[u]
        return pltpu.make_async_copy(sources[q][u], right.at[slot], right_sems.at[slot])

    def copy_left(s, m):
        eighth, span = s if fresh else table[n + s], pl.ds(m * tile, tile)
        return pltpu.make_async_copy(panel.at[eighth, span], left.at[s, span], left_sems.at[m, s])

    def window(ref, m, q, b):
        return ref.at[pl.ds(m * tile, tile), pl.ds((STREAMS * b + streams[q]) * width, width)]

    def copies_in(t):
        copies = [pltpu.make_async_copy(window(carried[0], *steps[t]), tiles.at[t], in_sems.at[0, t])]
        if fresh:
            copies.append(pltpu.make_async_copy(window(carried[1], *steps[t]), added.at[t], in_sems.at[1, t]))
        return copies

    def copy_out(t):
        return pltpu.make_async_copy(tiles.at[t], window(out, *steps[t]), out_sems.at[t])

    for s in range(eighths):
        copy_left(s, 0).start()
    lead = 1 if fresh else 3
    for t in range(lead):
        for copy in copies_in(t):
            copy.start()
    for q in range(len(streams)):
        for u in range(n):
            copy_right(q, u).start()
    for u in range(n):
        lookup[table[u]] = table[n + u] if fresh else u

    zeros = table[2 * n]
    for t, (m, q, b) in enumerate(steps):
        first = q == 0 and b == 0
        if first:
            for s in range(eighths):
                copy_left(s, m).wait()
        for copy in copies_in(t):
            copy.wait()
        if first and m + 1 < rows // tile:
            for s in range(eighths):
                copy_left(s, m + 1).start()
        if t + lead < len(steps):
            for copy in copies_in(t + lead):
                copy.start()
        if fresh:
            tiles[t] = 0.9 * tiles[t] + 0.1 * added[t].astype(jnp.float32)

        def pair(p, _):
            if m == 0:
                for s in range(2):
                    slot = q * n + 2 * p + s
                    pltpu.make_async_copy(sources[0][0], right.at[slot], right_sems.at[slot]).wait()
            parts = [
                lax.dot_general(
                    left[lookup[2 * p + s], m * tile : (m + 1) * tile, :],
                    right[q * n + 2 * p + s],
                    (((1,), (1,)), ((), ())),
                    preferred_element_type=jnp.float32,
                )
                for s in range(2)
            ]
            tiles[t] += 0.1 * (parts[0] + parts[1])
            return 0

        lax.fori_loop(0 if b == 0 else zeros // 2, zeros // 2 if b == 0 else n // 2, pair, 0)
        top = table[2 * n + 1] * rows + m * tile
        side = (table[2 * n + 2] * 2 + b) * (width * STREAMS) + streams[q] * width

        @pl.when(top < side + width - 1)
        def _():
            at_row = top + lax.broadcasted_iota(jnp.int32, (tile, width), 0)
            at_col = side + lax.broadcasted_iota(jnp.int32, (tile, width), 1)
            tiles[t] = jnp.where(at_row >= at_col, tiles[t], 0.0)

        copy_out(t).start()
    for t in range(len(steps)):
        copy_out(t).wait()


def blend(streams, pieces, table, panel, groups, fresh, before):
    eighths, rows, depth = panel.shape
    n, width = len(pieces[0]), groups[0].shape[1]
    held = n if fresh is None else eighths
    count = 2 * len(streams) * rows // ROWS_TILE
    carried = [before] if fresh is None else list(fresh)
    extra = [] if fresh is None or before is None else [before]
    operands = [table, panel, *groups, *carried, *extra]
    anywhere = pl.BlockSpec(memory_space=pl.ANY)
    return pl.pallas_call(
        functools.partial(blend_kernel, streams, pieces, fresh is not None),
        in_specs=[pl.BlockSpec(memory_space=pltpu.SMEM)] + [anywhere] * (len(operands) - 1),
        out_specs=anywhere,
        scratch_shapes=[
            pltpu.VMEM((held, rows, depth), jnp.bfloat16),
            pltpu.VMEM((len(streams) * n, width, depth), jnp.bfloat16),
            pltpu.VMEM((count, ROWS_TILE, width), jnp.float32),
            pltpu.VMEM((count if fresh else 1, ROWS_TILE, width), jnp.bfloat16),
            pltpu.SMEM((n,), jnp.int32),
            pltpu.SemaphoreType.DMA((rows // ROWS_TILE, held)),
            pltpu.SemaphoreType.DMA((len(streams) * n,)),
            pltpu.SemaphoreType.DMA((2, count)),
            pltpu.SemaphoreType.DMA((count,)),
        ],
        out_shape=jax.ShapeDtypeStruct((rows, 2 * STREAMS * width), jnp.float32),
        input_output_aliases={} if before is None else {len(operands) - 1: 0},
        compiler_params=pltpu.CompilerParams(vmem_limit_bytes=58 * 2**20),
        cost_estimate=pl.CostEstimate(
            flops=2 * len(streams) * n * rows * width * depth, bytes_accessed=24 * 2**20, transcendentals=0
        ),
    )(*operands)


def halves_kernel(ahead, behind, low, high, held, sems):
    count = low.shape[0]
    pairs = [(ahead.at[s], low.at[s]) for s in range(count)] + [(behind.at[count + s], high.at[s]) for s in range(count)]
    loads = [pltpu.make_async_copy(a, held.at[n], sems.at[0, n]) for n, (a, _) in enumerate(pairs)]
    stores = [pltpu.make_async_copy(held.at[n], b, sems.at[1, n]) for n, (_, b) in enumerate(pairs)]
    for load in loads:
        load.start()
    for load, store in zip(loads, stores):
        load.wait()
        store.start()
    for store in stores:
        store.wait()


def halves(ahead, behind):
    count, width, depth = ahead.shape
    half = jax.ShapeDtypeStruct((count // 2, width, depth), ahead.dtype)
    anywhere = pl.BlockSpec(memory_space=pl.ANY)
    return pl.pallas_call(
        halves_kernel,
        in_specs=[anywhere, anywhere],
        out_specs=[anywhere, anywhere],
        out_shape=[half, half],
        scratch_shapes=[pltpu.VMEM((count, width, depth), ahead.dtype), pltpu.SemaphoreType.DMA((2, count))],
        compiler_params=pltpu.CompilerParams(vmem_limit_bytes=58 * 2**20),
        cost_estimate=pl.CostEstimate(flops=0, bytes_accessed=4 * 2**20, transcendentals=0),
    )(ahead, behind)


def move(array, pairs):
    return lax.ppermute(array, AXES, pairs)


def shards(statistic, noise, grads):
    part = grads.shape[0] // STREAMS
    first = move(grads[:part], spread_pairs())
    first, rest = lax.optimization_barrier((first, grads))
    panel = lax.all_gather(rest, "col", axis=0)
    heads = [first, move(rest[part:], spread_pairs())]
    near, far = tables(unit_ids((0, 1, 3))), tables(unit_ids((2,)))
    inputs = (statistic, noise)

    def gather(unit):
        own = jnp.stack([unit] + [move(unit, shift_pairs(i, True)) for i in (1, -1, 2)])
        return own, move(own, shift_pairs(1, False)), move(own, shift_pairs(-1, False))

    def forward(ahead, behind):
        low, high = halves(ahead, behind)
        return move(low, shift_pairs(1, False)), move(high, shift_pairs(-1, False))

    held = [gather(unit) for unit in heads]
    units = [tuple((g, s) for g in range(3) for s in range(SIDE))]
    distant = forward(*held[0][1:])
    total = blend((0,), units, near, panel, held[0], inputs, None)
    (own, ahead, behind), total = lax.optimization_barrier((held[1], total))
    distant += forward(ahead, behind)
    total = blend((1,), units, near, panel, (own, ahead, behind), inputs, total)
    units = [tuple((2 * q + g, s) for g in range(2) for s in range(2)) for q in range(STREAMS)]
    return blend((0, 1), units, far, panel, distant, None, total)


def solution(mesh):
    in_specs = (P("row", "col"), P("row", "col"), P("row", "col"))
    out_specs = P("row", "col")
    return jax.shard_map(shards, mesh=mesh, in_specs=in_specs, out_specs=out_specs, check_vma=False)
```

```python
import functools

import jax
import jax.numpy as jnp
from jax import lax
from jax.experimental import pallas as pl
from jax.experimental.pallas import tpu as pltpu
from jax.sharding import PartitionSpec as P

AXES = ("row", "col")
SIDE = 4
ORDER = (0, 1, 3, 2)
ROWS_TILE = 512
STREAMS = 2


def place(y, x, z, core):
    return (y % SIDE * SIDE + x % SIDE) * 2 * SIDE + z % SIDE * 2 + core


def coords():
    for y in range(SIDE):
        for x in range(SIDE):
            for z in range(SIDE):
                for core in range(2):
                    yield y, x, z, core


def turn(t):
    return t if t % 2 else (t + 2) % SIDE


def spread_pairs():
    pairs = []
    for y, x, z, core in coords():
        half = x // 2
        to_x = x if core == half else SIDE - 1 - x
        pairs.append((place(y, x, z, core), place(y + turn((z - y) % SIDE), to_x, y, half)))
    return pairs


def shift_pairs(step, first):
    pairs = []
    for y, x, z, core in coords():
        along_x = (core == 0) == first
        to = place(y, x - step, z, core) if along_x else place(y - step, x, z, core)
        pairs.append((place(y, x, z, core), to))
    return pairs


def unit_ids(offsets):
    row, col = lax.axis_index("row"), lax.axis_index("col")
    y, x, z, core = row // SIDE, row % SIDE, col // 2, col % 2
    blocks, eighths = [], []
    for j in offsets:
        for i in ORDER:
            uy = (y + jnp.where(core == 0, j, i)) % SIDE
            ux = (x + jnp.where(core == 0, i, j)) % SIDE
            t = (uy - z) % SIDE
            k = (z + jnp.where(t % 2 == 1, t, (t + 2) % SIDE)) % SIDE
            home = ux // 2 == core
            source_x = jnp.where(home, ux, SIDE - 1 - ux)
            blocks.append(source_x % 2)
            eighths.append(2 * k + jnp.where(home, core, 1 - core))
    return blocks, eighths, [row, col]


def tables(held):
    blocks, eighths, place_ids = held
    ones = sum(blocks)
    zeros = len(blocks) - ones
    slots, seen = [], jnp.int32(0)
    for n, block in enumerate(blocks):
        slots.append(jnp.where(block == 1, zeros + seen, n - seen))
        seen = seen + block
    return jnp.stack(slots + eighths + [zeros] + place_ids).astype(jnp.int32)


def blend_kernel(streams, pieces, fresh, table, panel, *refs):
    count = 1 + max(g for units in pieces for g, _ in units)
    groups, refs = refs[:count], refs[count:]
    carried, refs = refs[: 2 if fresh else 1], refs[2 if fresh else 1 :]
    out, left, right, tiles, added, lookup, left_sems, right_sems, in_sems, out_sems = refs[-10:]
    sources = [[groups[g].at[s] for g, s in units] for units in pieces]
    n = len(sources[0])
    eighths, rows, depth = left.shape
    every = n >= panel.shape[0]
    width = right.shape[1]
    tile = tiles.shape[1]
    steps = [(m, q, b) for m in range(rows // tile) for q in range(len(streams)) for b in range(2)]

    def copy_right(q, u):
        slot = q * n + table[u]
        return pltpu.make_async_copy(sources[q][u], right.at[slot], right_sems.at[slot])

    def copy_left(s, m):
        eighth, span = s if every else table[n + s], pl.ds(m * tile, tile)
        return pltpu.make_async_copy(panel.at[eighth, span], left.at[s, span], left_sems.at[m, s])

    def window(ref, m, q, b):
        return ref.at[pl.ds(m * tile, tile), pl.ds((STREAMS * b + streams[q]) * width, width)]

    def copies_in(t):
        copies = [pltpu.make_async_copy(window(carried[0], *steps[t]), tiles.at[t], in_sems.at[0, t])]
        if fresh:
            copies.append(pltpu.make_async_copy(window(carried[1], *steps[t]), added.at[t], in_sems.at[1, t]))
        return copies

    def copy_out(t):
        return pltpu.make_async_copy(tiles.at[t], window(out, *steps[t]), out_sems.at[t])

    for s in range(eighths):
        copy_left(s, 0).start()
    lead = 1 if len(streams) == 1 else 3
    for t in range(lead):
        for copy in copies_in(t):
            copy.start()
    for q in range(len(streams)):
        for u in range(n):
            copy_right(q, u).start()
    for u in range(n):
        lookup[table[u]] = table[n + u] if every else u

    zeros = table[2 * n]
    for t, (m, q, b) in enumerate(steps):
        first = q == 0 and b == 0
        if first:
            for s in range(eighths):
                copy_left(s, m).wait()
        for copy in copies_in(t):
            copy.wait()
        if first and m + 1 < rows // tile:
            for s in range(eighths):
                copy_left(s, m + 1).start()
        if t + lead < len(steps):
            for copy in copies_in(t + lead):
                copy.start()
        if fresh:
            tiles[t] = 0.9 * tiles[t] + 0.1 * added[t].astype(jnp.float32)

        def pair(p, _):
            if m == 0:
                for s in range(2):
                    slot = q * n + 2 * p + s
                    pltpu.make_async_copy(sources[0][0], right.at[slot], right_sems.at[slot]).wait()
            parts = [
                lax.dot_general(
                    left[lookup[2 * p + s], m * tile : (m + 1) * tile, :],
                    right[q * n + 2 * p + s],
                    (((1,), (1,)), ((), ())),
                    preferred_element_type=jnp.float32,
                )
                for s in range(2)
            ]
            tiles[t] += 0.1 * (parts[0] + parts[1])
            return 0

        lax.fori_loop(0 if b == 0 else zeros // 2, zeros // 2 if b == 0 else n // 2, pair, 0)
        top = table[2 * n + 1] * rows + m * tile
        side = (table[2 * n + 2] * 2 + b) * (width * STREAMS) + streams[q] * width

        @pl.when(top < side + width - 1)
        def _():
            at_row = top + lax.broadcasted_iota(jnp.int32, (tile, width), 0)
            at_col = side + lax.broadcasted_iota(jnp.int32, (tile, width), 1)
            tiles[t] = jnp.where(at_row >= at_col, tiles[t], 0.0)

        copy_out(t).start()
    for t in range(len(steps)):
        copy_out(t).wait()


def blend(streams, pieces, table, panel, groups, fresh, before):
    eighths, rows, depth = panel.shape
    n, width = len(pieces[0]), groups[0].shape[1]
    held = min(n, eighths)
    count = 2 * len(streams) * rows // ROWS_TILE
    carried = [before] if fresh is None else list(fresh)
    extra = [] if fresh is None or before is None else [before]
    operands = [table, panel, *groups, *carried, *extra]
    anywhere = pl.BlockSpec(memory_space=pl.ANY)
    return pl.pallas_call(
        functools.partial(blend_kernel, streams, pieces, fresh is not None),
        in_specs=[pl.BlockSpec(memory_space=pltpu.SMEM)] + [anywhere] * (len(operands) - 1),
        out_specs=anywhere,
        scratch_shapes=[
            pltpu.VMEM((held, rows, depth), jnp.bfloat16),
            pltpu.VMEM((len(streams) * n, width, depth), jnp.bfloat16),
            pltpu.VMEM((count, ROWS_TILE, width), jnp.float32),
            pltpu.VMEM((count if fresh else 1, ROWS_TILE, width), jnp.bfloat16),
            pltpu.SMEM((n,), jnp.int32),
            pltpu.SemaphoreType.DMA((rows // ROWS_TILE, held)),
            pltpu.SemaphoreType.DMA((len(streams) * n,)),
            pltpu.SemaphoreType.DMA((2, count)),
            pltpu.SemaphoreType.DMA((count,)),
        ],
        out_shape=jax.ShapeDtypeStruct((rows, 2 * STREAMS * width), jnp.float32),
        input_output_aliases={} if before is None else {len(operands) - 1: 0},
        compiler_params=pltpu.CompilerParams(vmem_limit_bytes=58 * 2**20),
        cost_estimate=pl.CostEstimate(
            flops=2 * len(streams) * n * rows * width * depth, bytes_accessed=24 * 2**20, transcendentals=0
        ),
    )(*operands)


def halves_kernel(ahead, behind, low, high, held, sems):
    count = low.shape[0]
    pairs = [(ahead.at[s], low.at[s]) for s in range(count)] + [(behind.at[count + s], high.at[s]) for s in range(count)]
    loads = [pltpu.make_async_copy(a, held.at[n], sems.at[0, n]) for n, (a, _) in enumerate(pairs)]
    stores = [pltpu.make_async_copy(held.at[n], b, sems.at[1, n]) for n, (_, b) in enumerate(pairs)]
    for load in loads:
        load.start()
    for load, store in zip(loads, stores):
        load.wait()
        store.start()
    for store in stores:
        store.wait()


def halves(ahead, behind):
    count, width, depth = ahead.shape
    half = jax.ShapeDtypeStruct((count // 2, width, depth), ahead.dtype)
    anywhere = pl.BlockSpec(memory_space=pl.ANY)
    return pl.pallas_call(
        halves_kernel,
        in_specs=[anywhere, anywhere],
        out_specs=[anywhere, anywhere],
        out_shape=[half, half],
        scratch_shapes=[pltpu.VMEM((count, width, depth), ahead.dtype), pltpu.SemaphoreType.DMA((2, count))],
        compiler_params=pltpu.CompilerParams(vmem_limit_bytes=58 * 2**20),
        cost_estimate=pl.CostEstimate(flops=0, bytes_accessed=4 * 2**20, transcendentals=0),
    )(ahead, behind)


def move(array, pairs):
    return lax.ppermute(array, AXES, pairs)


def shards(statistic, noise, grads):
    part = grads.shape[0] // STREAMS
    first = move(grads[:part], spread_pairs())
    first, rest = lax.optimization_barrier((first, grads))
    panel = lax.all_gather(rest, "col", axis=0)
    heads = [first, move(rest[part:], spread_pairs())]
    mine, near, far = (tables(unit_ids(offsets)) for offsets in ((0,), (1, 3), (2,)))
    inputs = (statistic, noise)

    def gather(unit):
        own = jnp.stack([unit] + [move(unit, shift_pairs(i, True)) for i in (1, -1, 2)])
        return own, move(own, shift_pairs(1, False)), move(own, shift_pairs(-1, False))

    def forward(ahead, behind):
        low, high = halves(ahead, behind)
        return move(low, shift_pairs(1, False)), move(high, shift_pairs(-1, False))

    held = [gather(unit) for unit in heads]
    units = [tuple((q, s) for s in range(SIDE)) for q in range(STREAMS)]
    total = blend((0, 1), units, mine, panel, [own for own, _, _ in held], inputs, None)
    units = [tuple((g, s) for g in range(2) for s in range(SIDE))]
    distant = ()
    for stream, (_, ahead, behind) in enumerate(held):
        (ahead, behind), total = lax.optimization_barrier(((ahead, behind), total))
        distant += forward(ahead, behind)
        total = blend((stream,), units, near, panel, (ahead, behind), None, total)
    units = [tuple((2 * q + g, s) for g in range(2) for s in range(2)) for q in range(STREAMS)]
    return blend((0, 1), units, far, panel, distant, None, total)


def solution(mesh):
    in_specs = (P("row", "col"), P("row", "col"), P("row", "col"))
    out_specs = P("row", "col")
    return jax.shard_map(shards, mesh=mesh, in_specs=in_specs, out_specs=out_specs, check_vma=False)
```

```python
import functools

import jax
import jax.numpy as jnp
from jax import lax
from jax.experimental import pallas as pl
from jax.experimental.pallas import tpu as pltpu
from jax.sharding import PartitionSpec as P

AXES = ("row", "col")
SIDE = 4
ORDER = (0, 1, 3, 2)
ROWS_TILE = 512
STREAMS = 2


def place(y, x, z, core):
    return (y % SIDE * SIDE + x % SIDE) * 2 * SIDE + z % SIDE * 2 + core


def coords():
    for y in range(SIDE):
        for x in range(SIDE):
            for z in range(SIDE):
                for core in range(2):
                    yield y, x, z, core


def turn(t):
    return t if t % 2 else (t + 2) % SIDE


def spread_pairs():
    pairs = []
    for y, x, z, core in coords():
        half = x // 2
        to_x = x if core == half else SIDE - 1 - x
        pairs.append((place(y, x, z, core), place(y + turn((z - y) % SIDE), to_x, y, half)))
    return pairs


def shift_pairs(step, first):
    pairs = []
    for y, x, z, core in coords():
        along_x = (core == 0) == first
        to = place(y, x - step, z, core) if along_x else place(y - step, x, z, core)
        pairs.append((place(y, x, z, core), to))
    return pairs


def unit_ids(offsets):
    row, col = lax.axis_index("row"), lax.axis_index("col")
    y, x, z, core = row // SIDE, row % SIDE, col // 2, col % 2
    blocks, eighths = [], []
    for j in offsets:
        for i in ORDER:
            uy = (y + jnp.where(core == 0, j, i)) % SIDE
            ux = (x + jnp.where(core == 0, i, j)) % SIDE
            t = (uy - z) % SIDE
            k = (z + jnp.where(t % 2 == 1, t, (t + 2) % SIDE)) % SIDE
            home = ux // 2 == core
            source_x = jnp.where(home, ux, SIDE - 1 - ux)
            blocks.append(source_x % 2)
            eighths.append(2 * k + jnp.where(home, core, 1 - core))
    return blocks, eighths, [row, col]


def tables(held):
    blocks, eighths, place_ids = held
    ones = sum(blocks)
    zeros = len(blocks) - ones
    slots, seen = [], jnp.int32(0)
    for n, block in enumerate(blocks):
        slots.append(jnp.where(block == 1, zeros + seen, n - seen))
        seen = seen + block
    return jnp.stack(slots + eighths + [zeros] + place_ids).astype(jnp.int32)


def blend_kernel(streams, pieces, fresh, table, panel, *refs):
    count = 1 + max(g for units in pieces for g, _ in units)
    groups, refs = refs[:count], refs[count:]
    carried, refs = refs[: 2 if fresh else 1], refs[2 if fresh else 1 :]
    out, left, right, tiles, added, lookup, left_sems, right_sems, in_sems, out_sems = refs[-10:]
    sources = [[groups[g].at[s] for g, s in units] for units in pieces]
    n = len(sources[0])
    eighths, rows, depth = left.shape
    width = right.shape[1]
    tile = tiles.shape[1]
    steps = [(m, q, b) for m in range(rows // tile) for q in range(len(streams)) for b in range(2)]

    def copy_right(q, u):
        slot = q * n + table[u]
        return pltpu.make_async_copy(sources[q][u], right.at[slot], right_sems.at[slot])

    def copy_left(s, m):
        eighth, span = s if fresh else table[n + s], pl.ds(m * tile, tile)
        return pltpu.make_async_copy(panel.at[eighth, span], left.at[s, span], left_sems.at[m, s])

    def window(ref, m, q, b):
        return ref.at[pl.ds(m * tile, tile), pl.ds((STREAMS * b + streams[q]) * width, width)]

    def copies_in(t):
        copies = [pltpu.make_async_copy(window(carried[0], *steps[t]), tiles.at[t], in_sems.at[0, t])]
        if fresh:
            copies.append(pltpu.make_async_copy(window(carried[1], *steps[t]), added.at[t], in_sems.at[1, t]))
        return copies

    def copy_out(t):
        return pltpu.make_async_copy(tiles.at[t], window(out, *steps[t]), out_sems.at[t])

    for s in range(eighths):
        copy_left(s, 0).start()
    lead = 1 if fresh else 3
    for t in range(lead):
        for copy in copies_in(t):
            copy.start()
    for q in range(len(streams)):
        for u in range(n):
            copy_right(q, u).start()
    for u in range(n):
        lookup[table[u]] = table[n + u] if fresh else u

    zeros = table[2 * n]
    for t, (m, q, b) in enumerate(steps):
        first = q == 0 and b == 0
        if first:
            for s in range(eighths):
                copy_left(s, m).wait()
        for copy in copies_in(t):
            copy.wait()
        if first and m + 1 < rows // tile:
            for s in range(eighths):
                copy_left(s, m + 1).start()
        if t + lead < len(steps):
            for copy in copies_in(t + lead):
                copy.start()
        if fresh:
            tiles[t] = 0.9 * tiles[t] + 0.1 * added[t].astype(jnp.float32)

        def pair(p, _):
            if m == 0:
                for s in range(2):
                    slot = q * n + 2 * p + s
                    pltpu.make_async_copy(sources[0][0], right.at[slot], right_sems.at[slot]).wait()
            parts = [
                lax.dot_general(
                    left[lookup[2 * p + s], m * tile : (m + 1) * tile, :],
                    right[q * n + 2 * p + s],
                    (((1,), (1,)), ((), ())),
                    preferred_element_type=jnp.float32,
                )
                for s in range(2)
            ]
            tiles[t] += 0.1 * (parts[0] + parts[1])
            return 0

        lax.fori_loop(0 if b == 0 else zeros // 2, zeros // 2 if b == 0 else n // 2, pair, 0)
        top = table[2 * n + 1] * rows + m * tile
        side = (table[2 * n + 2] * 2 + b) * (width * STREAMS) + streams[q] * width

        @pl.when(top < side + width - 1)
        def _():
            at_row = top + lax.broadcasted_iota(jnp.int32, (tile, width), 0)
            at_col = side + lax.broadcasted_iota(jnp.int32, (tile, width), 1)
            tiles[t] = jnp.where(at_row >= at_col, tiles[t], 0.0)

        copy_out(t).start()
    for t in range(len(steps)):
        copy_out(t).wait()


def blend(streams, pieces, table, panel, groups, fresh, before):
    eighths, rows, depth = panel.shape
    n, width = len(pieces[0]), groups[0].shape[1]
    held = n if fresh is None else eighths
    count = 2 * len(streams) * rows // ROWS_TILE
    carried = [before] if fresh is None else list(fresh)
    extra = [] if fresh is None or before is None else [before]
    operands = [table, panel, *groups, *carried, *extra]
    anywhere = pl.BlockSpec(memory_space=pl.ANY)
    return pl.pallas_call(
        functools.partial(blend_kernel, streams, pieces, fresh is not None),
        in_specs=[pl.BlockSpec(memory_space=pltpu.SMEM)] + [anywhere] * (len(operands) - 1),
        out_specs=anywhere,
        scratch_shapes=[
            pltpu.VMEM((held, rows, depth), jnp.bfloat16),
            pltpu.VMEM((len(streams) * n, width, depth), jnp.bfloat16),
            pltpu.VMEM((count, ROWS_TILE, width), jnp.float32),
            pltpu.VMEM((count if fresh else 1, ROWS_TILE, width), jnp.bfloat16),
            pltpu.SMEM((n,), jnp.int32),
            pltpu.SemaphoreType.DMA((rows // ROWS_TILE, held)),
            pltpu.SemaphoreType.DMA((len(streams) * n,)),
            pltpu.SemaphoreType.DMA((2, count)),
            pltpu.SemaphoreType.DMA((count,)),
        ],
        out_shape=jax.ShapeDtypeStruct((rows, 2 * STREAMS * width), jnp.float32),
        input_output_aliases={} if before is None else {len(operands) - 1: 0},
        compiler_params=pltpu.CompilerParams(vmem_limit_bytes=(58 if len(streams) == 1 else 48) * 2**20),
        cost_estimate=pl.CostEstimate(
            flops=2 * len(streams) * n * rows * width * depth, bytes_accessed=24 * 2**20, transcendentals=0
        ),
    )(*operands)


def halves_kernel(ahead, behind, low, high, held, sems):
    count = low.shape[0]
    pairs = [(ahead.at[s], low.at[s]) for s in range(count)] + [(behind.at[count + s], high.at[s]) for s in range(count)]
    loads = [pltpu.make_async_copy(a, held.at[n], sems.at[0, n]) for n, (a, _) in enumerate(pairs)]
    stores = [pltpu.make_async_copy(held.at[n], b, sems.at[1, n]) for n, (_, b) in enumerate(pairs)]
    for load in loads:
        load.start()
    for load, store in zip(loads, stores):
        load.wait()
        store.start()
    for store in stores:
        store.wait()


def halves(ahead, behind):
    count, width, depth = ahead.shape
    half = jax.ShapeDtypeStruct((count // 2, width, depth), ahead.dtype)
    anywhere = pl.BlockSpec(memory_space=pl.ANY)
    return pl.pallas_call(
        halves_kernel,
        in_specs=[anywhere, anywhere],
        out_specs=[anywhere, anywhere],
        out_shape=[half, half],
        scratch_shapes=[pltpu.VMEM((count, width, depth), ahead.dtype), pltpu.SemaphoreType.DMA((2, count))],
        compiler_params=pltpu.CompilerParams(vmem_limit_bytes=58 * 2**20),
        cost_estimate=pl.CostEstimate(flops=0, bytes_accessed=4 * 2**20, transcendentals=0),
    )(ahead, behind)


def move(array, pairs):
    return lax.ppermute(array, AXES, pairs)


def shards(statistic, noise, grads):
    part = grads.shape[0] // STREAMS
    first = move(grads[:part], spread_pairs())
    first, rest = lax.optimization_barrier((first, grads))
    panel = lax.all_gather(rest, "col", axis=0)
    heads = [first, move(rest[part:], spread_pairs())]
    near, far = tables(unit_ids((0, 1, 3))), tables(unit_ids((2,)))
    inputs = (statistic, noise)

    def gather(unit):
        own = jnp.stack([unit] + [move(unit, shift_pairs(i, True)) for i in (1, -1, 2)])
        return own, move(own, shift_pairs(1, False)), move(own, shift_pairs(-1, False))

    def forward(ahead, behind):
        low, high = halves(ahead, behind)
        return move(low, shift_pairs(1, False)), move(high, shift_pairs(-1, False))

    held = [gather(unit) for unit in heads]
    units = [tuple((g, s) for g in range(3) for s in range(SIDE))]
    distant = forward(*held[0][1:])
    total = blend((0,), units, near, panel, held[0], inputs, None)
    (own, ahead, behind), total = lax.optimization_barrier((held[1], total))
    distant += forward(ahead, behind)
    total = blend((1,), units, near, panel, (own, ahead, behind), inputs, total)
    units = [tuple((2 * q + g, s) for g in range(2) for s in range(2)) for q in range(STREAMS)]
    return blend((0, 1), units, far, panel, distant, None, total)


def solution(mesh):
    in_specs = (P("row", "col"), P("row", "col"), P("row", "col"))
    out_specs = P("row", "col")
    return jax.shard_map(shards, mesh=mesh, in_specs=in_specs, out_specs=out_specs, check_vma=False)
```
